32 devices in a mesh: hst: 8 (over y, x, core), chip: 4 (over z).
Axes of the slice: x: 2, y: 2, z: 4, core: 2. Of those that a mesh axis runs over, the one named last changes fastest.
Arguments:
- points: bfloat16 [16384, 1024], P(('hst', 'chip')), may hold values from -640 to 640
- assign: int32 [16384], P(('hst', 'chip')), may hold values from 0 to 1023, as said below
Outputs:
- centroids: bfloat16 [1024, 1024], P('hst', 'chip')
- nearest: float32 [16384], P(('hst', 'chip'))
The draws below stay inside these ranges and needn't reach their ends.
Inputs may be any that keep to these rules, and one draw needn't show every extreme that they name: `assign`: cluster o * 128 + j lies in owner block o. Among the 512 points of one device at most 128 name clusters of any one owner block; in every draw one owner block gets exactly 128 points from every device.
All inputs are finite; a program needn't handle non-finite values.
Results may differ from the reference program's by a relative error of at most 0.0095.
Values may be sent and summed in bfloat16 or wider, within the bound.
A program may use at most 64 MiB of HBM per device.

```python
import math
import jax
import jax.numpy as jnp
from jax import lax

D = 1024
K_HOST = 128
P_DEV = 512
CYCLE = 8
K = 1024
POINTS = 16384
CAP = 128
N_HST = 8
N_CHIP = 4


def owner_table(key):
    slot_count = N_HST * CAP
    device_count = POINTS // P_DEV
    chosen = jax.random.randint(jax.random.fold_in(key, 11), (), 0, N_HST)

    def one_device(subkey):
        order_key, shuffle_key = jax.random.split(subkey)
        ordering = jax.random.permutation(order_key, slot_count)
        slot_owner = ordering // CAP
        ranking = jnp.where(slot_owner == chosen, 0, slot_count) + jnp.arange(slot_count)
        picked = slot_owner[jnp.argsort(ranking)[:P_DEV]]
        return picked[jax.random.permutation(shuffle_key, P_DEV)]
    device_keys = jax.random.split(jax.random.fold_in(key, 12), device_count)
    owners_all = jax.vmap(one_device)(device_keys).reshape(POINTS)
    within = jax.random.randint(jax.random.fold_in(key, 13), (POINTS,), 0, K_HOST)
    return (owners_all * K_HOST + within).astype(jnp.int32)


def draw_assign(key, part):
    return owner_table(key)


def draw_points(key, part):
    labels = owner_table(key)
    centres = jax.random.truncated_normal(jax.random.fold_in(key, 21), -4.0, 4.0, (K, D), jnp.float32)
    noise = jax.random.truncated_normal(jax.random.fold_in(key, 22), -4.0, 4.0, (POINTS, D), jnp.float32)
    column_scale = jnp.exp(jax.random.uniform(jax.random.fold_in(key, 23), (D,), jnp.float32, 0.0, math.log(10.0)))
    values = (1.5 * centres[labels] + noise) * column_scale[None, :]
    return values.astype(jnp.bfloat16)


def setup_inputs(seed: int = 0) -> dict:
    key_of = jax.random.split(jax.random.key(seed), 3)
    return {
        "points": draw_points(jax.random.fold_in(key_of[2], 71), 0),
        "assign": draw_assign(jax.random.fold_in(key_of[2], 71), 0),
    }


EPSILON = 1e-06

def reference(points, assign):
    host_rows = N_CHIP * P_DEV
    pieces = points.reshape(N_HST, host_rows, D)
    labels = assign.reshape(N_HST, host_rows)

    def add_host(running, item):
        values, groups = item
        return (running + jax.ops.segment_sum(values.astype(jnp.float32), groups, num_segments=K), None)
    sums, unused = lax.scan(add_host, jnp.zeros((K, D), jnp.float32), (pieces, labels))
    factor = lax.rsqrt(lax.optimization_barrier(jnp.mean(sums * sums, axis=1, keepdims=True)) + EPSILON)
    centroids = (sums * factor).astype(jnp.bfloat16)
    blocks = centroids.reshape(N_HST, K_HOST, D)

    def host_nearest(host_index):
        widened = pieces[host_index].astype(jnp.float32)
        unit_points = (widened * lax.rsqrt(lax.optimization_barrier(jnp.mean(widened * widened, axis=1, keepdims=True)) + EPSILON)).astype(jnp.bfloat16)
        chosen = (host_index - jnp.arange(CYCLE, dtype=jnp.int32)) % N_HST
        window = blocks[chosen].reshape(CYCLE * K_HOST, D)
        scores = jnp.einsum('pd,kd->pk', unit_points.astype(jnp.float32), window.astype(jnp.float32))
        return lax.optimization_barrier(jnp.min(2.0 - 2.0 * scores / D, axis=1))
    nearest = lax.map(host_nearest, jnp.arange(N_HST, dtype=jnp.int32)).reshape(POINTS)
    return (centroids, nearest)
```

```python
import functools

import jax
import jax.numpy as jnp
from jax import lax
from jax.experimental import pallas as pl
from jax.experimental.pallas import tpu as pltpu
from jax.sharding import PartitionSpec as P

K_HOST = 128
CYCLE = 8


EPSILON = 1e-06
MESH = pl.DeviceIdType.MESH


def shifted(block, axis, distance):
    devices = range(lax.axis_size(axis))
    route = [((i - distance) % len(devices), i) for i in devices]
    return lax.ppermute(block, axis, route)


def cluster_sums(values, labels, row_count):
    stride = min(row_count, 1024)

    def one_block(offset):
        wanted = offset + jnp.arange(stride, dtype=jnp.int32)
        member = (wanted[:, None] == labels[None, :]).astype(jnp.bfloat16)
        return jnp.dot(member, values, preferred_element_type=jnp.float32)

    offsets = jnp.arange(row_count // stride, dtype=jnp.int32) * stride
    return lax.map(one_block, offsets).reshape(row_count, values.shape[1])


def general_body(points, assign):
    feature_count = points.shape[1]
    chip_count = lax.axis_size("chip")
    chip_index = lax.axis_index("chip")
    quarter = feature_count // chip_count
    host_points, host_labels = (
        lax.all_gather(points, "chip", axis=0, tiled=True),
        lax.all_gather(assign, "chip", axis=0, tiled=True),
    )
    columns = lax.dynamic_slice_in_dim(host_points, chip_index * quarter, quarter, 1)
    shares = lax.psum_scatter(
        cluster_sums(columns, host_labels, K_HOST * lax.axis_size("hst")),
        "hst",
        scatter_dimension=0,
        tiled=True,
    )
    squares = lax.psum(jnp.sum(shares * shares, axis=1), "chip")
    factor = lax.rsqrt(squares / feature_count + EPSILON)
    centroids = (shares * factor[:, None]).astype(jnp.bfloat16)
    own_block = lax.all_gather(centroids, "chip", axis=1, tiled=True)
    widened = points.astype(jnp.float32)
    unit_points = (
        widened * lax.rsqrt(jnp.mean(widened * widened, axis=1, keepdims=True) + EPSILON)
    ).astype(jnp.bfloat16)

    def nearest_in(candidates):
        scores = jnp.einsum(
            "pd,kd->pk", unit_points, candidates, preferred_element_type=jnp.float32
        )
        return jnp.min(2.0 - 2.0 * scores / feature_count, axis=1)

    nearest = nearest_in(own_block)
    moving = own_block
    for section_index in range(CYCLE - 1):
        moving = shifted(moving, "hst", 1)
        nearest = jnp.minimum(nearest, nearest_in(moving))
    return (centroids, nearest)


QUAD = 4


def window_kernel(
    chips,
    lab_ref,
    pts_ref,
    cent_ref,
    near_ref,
    sib_lab,
    sib_pts,
    kept,
    out1,
    in1,
    out2,
    in2,
    grid,
    unit_t,
    best_out,
    best_in,
    core_send,
    core_recv,
    s1_send,
    s1_recv,
    s2_send,
    s2_recv,
    g1_send,
    g1_recv,
    g2_send,
    g2_recv,
):
    local, features = pts_ref.shape
    rows = K_HOST // chips
    h = lax.axis_index("hst")
    c = lax.axis_index("chip")
    core = h % 2
    quad = h // 2
    qx, qy = quad % 2, quad // 2
    sibling = (h + 1 - 2 * core, c)
    quads = [quad, qy * 2 + (1 - qx), (1 - qy) * 2 + qx, (1 - qy) * 2 + (1 - qx)]
    quad_ids = [(q * 2 + core, c) for q in quads]
    line = [(c + d) % chips for d in range(chips)]
    line_ids = [(h, k) for k in line]

    barrier = pltpu.get_barrier_semaphore()
    partners = [sibling] + quad_ids[1:] + line_ids[1:]
    for partner in partners:
        pl.semaphore_signal(barrier, inc=1, device_id=partner, device_id_type=MESH)
    pl.semaphore_wait(barrier, len(partners))

    def remote(src, dst, send, recv, device):
        return pltpu.make_async_remote_copy(
            src_ref=src,
            dst_ref=dst,
            send_sem=send,
            recv_sem=recv,
            device_id=device,
            device_id_type=MESH,
        )

    lab_copy = remote(lab_ref, sib_lab, core_send.at[0], core_recv.at[0], sibling)
    lab_copy.start()
    pts_copy = remote(pts_ref, sib_pts, core_send.at[1], core_recv.at[1], sibling)
    pts_copy.start()
    lab_copy.wait_recv()
    pts_copy.wait_recv()

    order = [d % chips for d in range(1, chips + 1)]
    row = lax.broadcasted_iota(jnp.int32, (QUAD * rows, local), 0)
    part, within = row // rows, row % rows
    base = jnp.zeros_like(row)
    for r in range(QUAD):
        base = jnp.where(part == r, (quads[r] * 2 + core) * K_HOST, base)
    base = base + within
    first = [[None] * QUAD for _ in range(chips)]
    for s, d in enumerate(order):
        wanted = base + line[d] * rows
        mine = (wanted == lab_ref[...]).astype(jnp.bfloat16)
        theirs = (wanted == sib_lab[...]).astype(jnp.bfloat16)
        sums = jnp.dot(mine, pts_ref[...], preferred_element_type=jnp.float32)
        sums += jnp.dot(theirs, sib_pts[...], preferred_element_type=jnp.float32)
        kept[s] = sums[:rows]
        for r in range(1, QUAD):
            out1[s, r - 1] = sums[r * rows : (r + 1) * rows].astype(jnp.bfloat16)
            first[s][r] = remote(
                out1.at[s, r - 1],
                in1.at[s, r - 1],
                s1_send.at[s, r - 1],
                s1_recv.at[s, r - 1],
                quad_ids[r],
            )
            first[s][r].start()

    step = 128
    for side, ref in enumerate((pts_ref, sib_pts)):
        for begin in range(0, local, step):
            wide = ref[begin : begin + step].astype(jnp.float32)
            mean = jnp.mean(wide * wide, axis=1, keepdims=True)
            unit = wide * lax.rsqrt(mean + EPSILON)
            at = side * local + begin
            unit_t[:, at : at + step] = unit.T.astype(jnp.bfloat16)

    second = [None] * chips
    total = None
    for s, d in enumerate(order):
        total = kept[s]
        for r in range(1, QUAD):
            first[s][r].wait_recv()
            total = total + in1[s, r - 1].astype(jnp.float32)
        if d:
            out2[d - 1] = total.astype(jnp.bfloat16)
            second[d] = remote(
                out2.at[d - 1], in2.at[d - 1], s2_send.at[d - 1], s2_recv.at[d - 1], line_ids[d]
            )
            second[d].start()
    for d in range(1, chips):
        second[d].wait_recv()
        total = total + in2[d - 1].astype(jnp.float32)
    mean = jnp.mean(total * total, axis=1, keepdims=True)
    grid[0, c] = (total * lax.rsqrt(mean + EPSILON)).astype(jnp.bfloat16)

    along = [None] * chips
    for d in range(1, chips):
        along[d] = remote(
            grid.at[0, c], grid.at[0, c], g1_send.at[d - 1], g1_recv.at[d - 1], line_ids[d]
        )
        along[d].start()
    across = [[None] * QUAD for _ in range(chips)]
    for d in range(chips):
        if d:
            along[d].wait_recv()
        k = (c + chips - d) % chips
        for r in range(1, QUAD):
            across[d][r] = remote(
                grid.at[0, k], grid.at[r, k], g2_send.at[d, r - 1], g2_recv.at[d, r - 1], quad_ids[r]
            )
            across[d][r].start()

    def best_of(r):
        block = grid[r].reshape(K_HOST, features)
        scores = jnp.dot(block, unit_t[...], preferred_element_type=jnp.float32)
        return jnp.max(scores, axis=0, keepdims=True)

    quarter = features // chips
    columns = pl.ds(pl.multiple_of(c * quarter, quarter), quarter)
    for k in range(chips):
        cent_ref[k * rows : (k + 1) * rows, :] = grid[0, k, :, columns]
    best = best_of(0)
    for r in range(1, QUAD):
        for d in range(chips):
            across[d][r].wait_recv()
        best = jnp.maximum(best, best_of(r))

    best_out[...] = best[:, local:]
    last = remote(best_out, best_in, core_send.at[2], core_recv.at[2], sibling)
    last.start()
    for s in range(chips):
        for r in range(1, QUAD):
            first[s][r].wait_send()
            across[s][r].wait_send()
    for d in range(1, chips):
        second[d].wait_send()
        along[d].wait_send()
    lab_copy.wait_send()
    pts_copy.wait_send()
    last.wait()
    near_ref[...] = 2.0 - 2.0 * jnp.maximum(best[:, :local], best_in[...]) / features


def window_body(points, assign):
    local, features = points.shape
    chips = lax.axis_size("chip")
    rows = K_HOST // chips
    vmem = pl.BlockSpec(memory_space=pltpu.VMEM)
    dma = pltpu.SemaphoreType.DMA
    centroids, nearest = pl.pallas_call(
        functools.partial(window_kernel, chips),
        out_shape=(
            jax.ShapeDtypeStruct((K_HOST, features // chips), jnp.bfloat16),
            jax.ShapeDtypeStruct((1, local), jnp.float32),
        ),
        in_specs=[vmem, vmem],
        out_specs=(vmem, vmem),
        scratch_shapes=[
            pltpu.VMEM((1, local), jnp.int32),
            pltpu.VMEM((local, features), jnp.bfloat16),
            pltpu.VMEM((chips, rows, features), jnp.float32),
            pltpu.VMEM((chips, QUAD - 1, rows, features), jnp.bfloat16),
            pltpu.VMEM((chips, QUAD - 1, rows, features), jnp.bfloat16),
            pltpu.VMEM((chips - 1, rows, features), jnp.bfloat16),
            pltpu.VMEM((chips - 1, rows, features), jnp.bfloat16),
            pltpu.VMEM((QUAD, chips, rows, features), jnp.bfloat16),
            pltpu.VMEM((features, 2 * local), jnp.bfloat16),
            pltpu.VMEM((1, local), jnp.float32),
            pltpu.VMEM((1, local), jnp.float32),
            dma((3,)),
            dma((3,)),
            dma((chips, QUAD - 1)),
            dma((chips, QUAD - 1)),
            dma((chips - 1,)),
            dma((chips - 1,)),
            dma((chips - 1,)),
            dma((chips - 1,)),
            dma((chips, QUAD - 1)),
            dma((chips, QUAD - 1)),
        ],
        compiler_params=pltpu.CompilerParams(
            collective_id=0, has_side_effects=True, vmem_limit_bytes=48 * 1024 * 1024
        ),
    )(assign.reshape(1, local), points)
    return (centroids, nearest.reshape(local))


def solution(mesh):
    hosts, chips = mesh.shape["hst"], mesh.shape["chip"]
    fits = hosts == CYCLE and hosts == 2 * QUAD and chips > 1 and K_HOST % (16 * chips) == 0
    in_specs = (P(("hst", "chip"), None), P(("hst", "chip")))
    out_specs = (P("hst", "chip"), P(("hst", "chip")))
    return jax.shard_map(
        window_body if fits else general_body,
        mesh=mesh,
        in_specs=in_specs,
        out_specs=out_specs,
        check_vma=False,
    )
```

```python
import functools

import jax
import jax.numpy as jnp
from jax import lax
from jax.experimental import pallas as pl
from jax.experimental.pallas import tpu as pltpu
from jax.sharding import PartitionSpec as P

K_HOST = 128
CYCLE = 8


EPSILON = 1e-06
MESH = pl.DeviceIdType.MESH


def shifted(block, axis, distance):
    devices = range(lax.axis_size(axis))
    route = [((i - distance) % len(devices), i) for i in devices]
    return lax.ppermute(block, axis, route)


def cluster_sums(values, labels, row_count):
    stride = min(row_count, 1024)

    def one_block(offset):
        wanted = offset + jnp.arange(stride, dtype=jnp.int32)
        member = (wanted[:, None] == labels[None, :]).astype(jnp.bfloat16)
        return jnp.dot(member, values, preferred_element_type=jnp.float32)

    offsets = jnp.arange(row_count // stride, dtype=jnp.int32) * stride
    return lax.map(one_block, offsets).reshape(row_count, values.shape[1])


def general_body(points, assign):
    feature_count = points.shape[1]
    chip_count = lax.axis_size("chip")
    chip_index = lax.axis_index("chip")
    quarter = feature_count // chip_count
    host_points, host_labels = (
        lax.all_gather(points, "chip", axis=0, tiled=True),
        lax.all_gather(assign, "chip", axis=0, tiled=True),
    )
    columns = lax.dynamic_slice_in_dim(host_points, chip_index * quarter, quarter, 1)
    shares = lax.psum_scatter(
        cluster_sums(columns, host_labels, K_HOST * lax.axis_size("hst")),
        "hst",
        scatter_dimension=0,
        tiled=True,
    )
    squares = lax.psum(jnp.sum(shares * shares, axis=1), "chip")
    factor = lax.rsqrt(squares / feature_count + EPSILON)
    centroids = (shares * factor[:, None]).astype(jnp.bfloat16)
    own_block = lax.all_gather(centroids, "chip", axis=1, tiled=True)
    widened = points.astype(jnp.float32)
    unit_points = (
        widened * lax.rsqrt(jnp.mean(widened * widened, axis=1, keepdims=True) + EPSILON)
    ).astype(jnp.bfloat16)

    def nearest_in(candidates):
        scores = jnp.einsum(
            "pd,kd->pk", unit_points, candidates, preferred_element_type=jnp.float32
        )
        return jnp.min(2.0 - 2.0 * scores / feature_count, axis=1)

    nearest = nearest_in(own_block)
    moving = own_block
    for section_index in range(CYCLE - 1):
        moving = shifted(moving, "hst", 1)
        nearest = jnp.minimum(nearest, nearest_in(moving))
    return (centroids, nearest)


QUAD = 4


def window_kernel(
    chips,
    lab_hbm,
    pts_hbm,
    cent_ref,
    near_ref,
    lab,
    pts,
    sib_lab,
    sib_pts,
    sums,
    out1,
    in1,
    out2,
    in2,
    out3,
    in3,
    grid,
    unit_t,
    best_out,
    best_in,
    load_sem,
    core_send,
    core_recv,
    s1_send,
    s1_recv,
    s2_send,
    s2_recv,
    s3_send,
    s3_recv,
    g1_send,
    g1_recv,
    g2_send,
    g2_recv,
    g3_send,
    g3_recv,
):
    local, features = pts.shape
    rows = K_HOST // chips
    half = features // 2
    halves = (slice(0, half), slice(half, features))
    h = lax.axis_index("hst")
    c = lax.axis_index("chip")
    core = h % 2
    quad = h // 2
    qx, qy = quad % 2, quad // 2
    sibling = (h + 1 - 2 * core, c)
    quads = [quad, qy * 2 + (1 - qx), (1 - qy) * 2 + qx, (1 - qy) * 2 + (1 - qx)]
    x_id, y_id = [(quads[r] * 2 + core, c) for r in (1, 2)]
    line = [c, c + 1 - 2 * (c % 2), (c + 2) % 4, 3 - c]
    line_ids = [(h, k) for k in line]

    barrier = pltpu.get_barrier_semaphore()
    partners = [sibling, x_id, y_id] + line_ids[1:]
    for partner in partners:
        pl.semaphore_signal(barrier, inc=1, device_id=partner, device_id_type=MESH)
    lab_load = pltpu.make_async_copy(lab_hbm, lab, load_sem.at[0])
    lab_load.start()
    pts_load = pltpu.make_async_copy(pts_hbm, pts, load_sem.at[1])
    pts_load.start()
    pl.semaphore_wait(barrier, len(partners))

    started = []

    def remote(src, dst, send, recv, device):
        copy = pltpu.make_async_remote_copy(
            src_ref=src,
            dst_ref=dst,
            send_sem=send,
            recv_sem=recv,
            device_id=device,
            device_id_type=MESH,
        )
        copy.start()
        started.append(copy)
        return copy

    lab_swap = remote(lab_hbm, sib_lab, core_send.at[0], core_recv.at[0], sibling)
    pts_swap = [
        remote(
            pts_hbm.at[:, halves[f]], sib_pts.at[:, halves[f]], core_send.at[1 + f], core_recv.at[1 + f], sibling
        )
        for f in range(2)
    ]

    order = (2, 3, 1, 0)
    row = lax.broadcasted_iota(jnp.int32, (QUAD * rows, local), 0)
    part, within = row // rows, row % rows
    base = jnp.zeros_like(row)
    for r in range(QUAD):
        base = jnp.where(part == r, (quads[r] * 2 + core) * K_HOST, base)
    base = base + within

    def members(s, labels):
        return (base + line[order[s]] * rows == labels[...]).astype(jnp.bfloat16)

    lab_load.wait()
    pts_load.wait()
    for s in range(chips):
        sums[s] = jnp.dot(members(s, lab), pts[...], preferred_element_type=jnp.float32)
    lab_swap.wait_recv()

    def piece(s, r, f):
        return sums[s, r * rows : (r + 1) * rows, halves[f]]

    first = [[None, None] for _ in range(chips)]
    second = [[None, None] for _ in range(chips)]
    third = [None] * chips

    def add_sibling(s):
        theirs = members(s, sib_lab)
        for f in range(2):
            if s == 0:
                pts_swap[f].wait_recv()
            sums[s, :, halves[f]] += jnp.dot(
                theirs, sib_pts[:, halves[f]], preferred_element_type=jnp.float32
            )
            near = 1 + f
            out1[s, f, 0] = piece(s, near, f).astype(jnp.bfloat16)
            out1[s, f, 1] = piece(s, 3, f).astype(jnp.bfloat16)
            if s < 2:
                send_first(s, f)

    def send_first(s, f):
        first[s][f] = remote(
            out1.at[s, f], in1.at[s, f], s1_send.at[s, f], s1_recv.at[s, f], (x_id, y_id)[f]
        )

    def send_second(s):
        for f in range(2):
            first[s][f].wait_recv()
            far = 2 - f
            out2[s, f] = (piece(s, far, f) + in1[s, f, 1].astype(jnp.float32)).astype(jnp.bfloat16)
            second[s][f] = remote(
                out2.at[s, f], in2.at[s, f], s2_send.at[s, f], s2_recv.at[s, f], (y_id, x_id)[f]
            )

    def finish(s):
        whole = []
        for f in range(2):
            second[s][f].wait_recv()
            whole.append(
                piece(s, 0, f) + in1[s, f, 0].astype(jnp.float32) + in2[s, f].astype(jnp.float32)
            )
        return jnp.concatenate(whole, axis=1)

    def send_third(s):
        m = order[s]
        out3[m - 1] = finish(s).astype(jnp.bfloat16)
        third[m] = remote(
            out3.at[m - 1], in3.at[m - 1], s3_send.at[m - 1], s3_recv.at[m - 1], line_ids[m]
        )

    step = 128

    def make_unit(index):
        at = index * step
        ref, begin = (pts, at) if at < local else (sib_pts, at - local)
        wide = ref[begin : begin + step].astype(jnp.float32)
        mean = jnp.mean(wide * wide, axis=1, keepdims=True)
        unit = wide * lax.rsqrt(mean + EPSILON)
        unit_t[:, at : at + step] = unit.T.astype(jnp.bfloat16)

    units = 2 * local // step
    for s in range(chips):
        add_sibling(s)
    made = 0
    for s in range(chips):
        for _ in range(units // chips):
            make_unit(made)
            made += 1
        send_second(s)
        if s + 2 < chips:
            send_first(s + 2, 0)
            send_first(s + 2, 1)
        if s:
            send_third(s - 1)
    total = finish(chips - 1)
    for m in (2, 3, 1):
        third[m].wait_recv()
        total = total + in3[m - 1].astype(jnp.float32)
    mean = jnp.mean(total * total, axis=1, keepdims=True)
    grid[0, c] = (total * lax.rsqrt(mean + EPSILON)).astype(jnp.bfloat16)

    along = [None] * chips
    across = [[None, None] for _ in range(chips)]
    corner = [[None, None] for _ in range(chips)]

    def send_across(m):
        k = line[m]
        for f in range(2):
            across[m][f] = remote(
                grid.at[0, k], grid.at[1 + f, k], g2_send.at[m, f], g2_recv.at[m, f], (x_id, y_id)[f]
            )

    def send_corner(m):
        k = line[m]
        for f in range(2):
            across[m][f].wait_recv()
            corner[m][f] = remote(
                grid.at[1 + f, k, :, halves[f]],
                grid.at[3, k, :, halves[f]],
                g3_send.at[m, f],
                g3_recv.at[m, f],
                (y_id, x_id)[f],
            )

    for m in range(1, chips):
        along[m] = remote(
            grid.at[0, c], grid.at[0, c], g1_send.at[m - 1], g1_recv.at[m - 1], line_ids[m]
        )
    send_across(0)
    for m in range(1, chips):
        along[m].wait_recv()
        send_across(m)
        send_corner(m - 1)

    def best_of(r):
        block = grid[r].reshape(K_HOST, features)
        scores = jnp.dot(block, unit_t[...], preferred_element_type=jnp.float32)
        return jnp.max(scores, axis=0, keepdims=True)

    quarter = features // chips
    columns = pl.ds(pl.multiple_of(c * quarter, quarter), quarter)
    for k in range(chips):
        cent_ref[k * rows : (k + 1) * rows, :] = grid[0, k, :, columns]
    best = best_of(0)
    send_corner(chips - 1)
    for r in (1, 2):
        best = jnp.maximum(best, best_of(r))
    for m in range(chips):
        for f in range(2):
            corner[m][f].wait_recv()
    best = jnp.maximum(best, best_of(3))

    best_out[...] = best[:, local:]
    last = remote(best_out, best_in, core_send.at[3], core_recv.at[3], sibling)
    for copy in started:
        copy.wait_send()
    last.wait_recv()
    near_ref[...] = 2.0 - 2.0 * jnp.maximum(best[:, :local], best_in[...]) / features


def window_body(points, assign):
    local, features = points.shape
    chips = lax.axis_size("chip")
    rows = K_HOST // chips
    half = features // 2
    vmem = pl.BlockSpec(memory_space=pltpu.VMEM)
    anywhere = pl.BlockSpec(memory_space=pl.ANY)
    dma = pltpu.SemaphoreType.DMA
    pieces = [
        pltpu.VMEM((chips, 2, 2, rows, half), jnp.bfloat16),
        pltpu.VMEM((chips, 2, rows, half), jnp.bfloat16),
        pltpu.VMEM((chips - 1, rows, features), jnp.bfloat16),
    ]
    pairs = [(4,), (chips, 2), (chips, 2), (chips - 1,), (chips - 1,), (chips, 2), (chips, 2)]
    centroids, nearest = pl.pallas_call(
        functools.partial(window_kernel, chips),
        out_shape=(
            jax.ShapeDtypeStruct((K_HOST, features // chips), jnp.bfloat16),
            jax.ShapeDtypeStruct((1, local), jnp.float32),
        ),
        in_specs=[anywhere, anywhere],
        out_specs=(vmem, vmem),
        scratch_shapes=[
            pltpu.VMEM((1, local), jnp.int32),
            pltpu.VMEM((local, features), jnp.bfloat16),
            pltpu.VMEM((1, local), jnp.int32),
            pltpu.VMEM((local, features), jnp.bfloat16),
            pltpu.VMEM((chips, QUAD * rows, features), jnp.float32),
            *(buffer for buffer in pieces for _ in range(2)),
            pltpu.VMEM((QUAD, chips, rows, features), jnp.bfloat16),
            pltpu.VMEM((features, 2 * local), jnp.bfloat16),
            pltpu.VMEM((1, local), jnp.float32),
            pltpu.VMEM((1, local), jnp.float32),
            dma((2,)),
            *(dma(shape) for shape in pairs for _ in range(2)),
        ],
        compiler_params=pltpu.CompilerParams(
            collective_id=0, has_side_effects=True, vmem_limit_bytes=48 * 1024 * 1024
        ),
    )(assign.reshape(1, local), points)
    return (centroids, nearest.reshape(local))


def solution(mesh):
    hosts, chips = mesh.shape["hst"], mesh.shape["chip"]
    fits = hosts == CYCLE and hosts == 2 * QUAD and chips == 4
    in_specs = (P(("hst", "chip"), None), P(("hst", "chip")))
    out_specs = (P("hst", "chip"), P(("hst", "chip")))
    return jax.shard_map(
        window_body if fits else general_body,
        mesh=mesh,
        in_specs=in_specs,
        out_specs=out_specs,
        check_vma=False,
    )
```

```python
import functools

import jax
import jax.numpy as jnp
from jax import lax
from jax.experimental import pallas as pl
from jax.experimental.pallas import tpu as pltpu
from jax.sharding import PartitionSpec as P

K_HOST = 128
CYCLE = 8


EPSILON = 1e-06
MESH = pl.DeviceIdType.MESH


def shifted(block, axis, distance):
    devices = range(lax.axis_size(axis))
    route = [((i - distance) % len(devices), i) for i in devices]
    return lax.ppermute(block, axis, route)


def cluster_sums(values, labels, row_count):
    stride = min(row_count, 1024)

    def one_block(offset):
        wanted = offset + jnp.arange(stride, dtype=jnp.int32)
        member = (wanted[:, None] == labels[None, :]).astype(jnp.bfloat16)
        return jnp.dot(member, values, preferred_element_type=jnp.float32)

    offsets = jnp.arange(row_count // stride, dtype=jnp.int32) * stride
    return lax.map(one_block, offsets).reshape(row_count, values.shape[1])


def general_body(points, assign):
    feature_count = points.shape[1]
    chip_count = lax.axis_size("chip")
    chip_index = lax.axis_index("chip")
    quarter = feature_count // chip_count
    host_points, host_labels = (
        lax.all_gather(points, "chip", axis=0, tiled=True),
        lax.all_gather(assign, "chip", axis=0, tiled=True),
    )
    columns = lax.dynamic_slice_in_dim(host_points, chip_index * quarter, quarter, 1)
    shares = lax.psum_scatter(
        cluster_sums(columns, host_labels, K_HOST * lax.axis_size("hst")),
        "hst",
        scatter_dimension=0,
        tiled=True,
    )
    squares = lax.psum(jnp.sum(shares * shares, axis=1), "chip")
    factor = lax.rsqrt(squares / feature_count + EPSILON)
    centroids = (shares * factor[:, None]).astype(jnp.bfloat16)
    own_block = lax.all_gather(centroids, "chip", axis=1, tiled=True)
    widened = points.astype(jnp.float32)
    unit_points = (
        widened * lax.rsqrt(jnp.mean(widened * widened, axis=1, keepdims=True) + EPSILON)
    ).astype(jnp.bfloat16)

    def nearest_in(candidates):
        scores = jnp.einsum(
            "pd,kd->pk", unit_points, candidates, preferred_element_type=jnp.float32
        )
        return jnp.min(2.0 - 2.0 * scores / feature_count, axis=1)

    nearest = nearest_in(own_block)
    moving = own_block
    for section_index in range(CYCLE - 1):
        moving = shifted(moving, "hst", 1)
        nearest = jnp.minimum(nearest, nearest_in(moving))
    return (centroids, nearest)


QUAD = 4


def window_kernel(
    chips,
    lab,
    pts,
    cent_ref,
    near_ref,
    sib_lab,
    sib_pts,
    sums,
    out1,
    in1,
    out2,
    in2,
    out3,
    in3,
    grid,
    unit_t,
    best_out,
    best_in,
    core_send,
    core_recv,
    s1_send,
    s1_recv,
    s2_send,
    s2_recv,
    s3_send,
    s3_recv,
    g1_send,
    g1_recv,
    g2_send,
    g2_recv,
):
    local, features = pts.shape
    rows = K_HOST // chips
    half = features // 2
    halves = (slice(0, half), slice(half, features))
    h = lax.axis_index("hst")
    c = lax.axis_index("chip")
    core = h % 2
    quad = h // 2
    qx, qy = quad % 2, quad // 2
    sibling = (h + 1 - 2 * core, c)
    quads = [quad, qy * 2 + (1 - qx), (1 - qy) * 2 + qx, (1 - qy) * 2 + (1 - qx)]
    quad_ids = [(q * 2 + core, c) for q in quads]
    x_id, y_id = quad_ids[1:3]
    line = [c, c + 1 - 2 * (c % 2), (c + 2) % 4, 3 - c]
    line_ids = [(h, k) for k in line]

    barrier = pltpu.get_barrier_semaphore()
    partners = [sibling] + quad_ids[1:] + line_ids[1:]
    for partner in partners:
        pl.semaphore_signal(barrier, inc=1, device_id=partner, device_id_type=MESH)
    pl.semaphore_wait(barrier, len(partners))

    started = []

    def remote(src, dst, send, recv, device):
        copy = pltpu.make_async_remote_copy(
            src_ref=src,
            dst_ref=dst,
            send_sem=send,
            recv_sem=recv,
            device_id=device,
            device_id_type=MESH,
        )
        copy.start()
        started.append(copy)
        return copy

    lab_swap = remote(lab, sib_lab, core_send.at[0], core_recv.at[0], sibling)
    pts_swap = [
        remote(
            pts.at[:, halves[f]], sib_pts.at[:, halves[f]], core_send.at[1 + f], core_recv.at[1 + f], sibling
        )
        for f in range(2)
    ]

    order = (2, 3, 1, 0)
    row = lax.broadcasted_iota(jnp.int32, (QUAD * rows, local), 0)
    part, within = row // rows, row % rows
    base = jnp.zeros_like(row)
    for r in range(QUAD):
        base = jnp.where(part == r, (quads[r] * 2 + core) * K_HOST, base)
    base = base + within

    def members(s, labels):
        return (base + line[order[s]] * rows == labels[...]).astype(jnp.bfloat16)

    for s in range(chips):
        sums[s] = jnp.dot(members(s, lab), pts[...], preferred_element_type=jnp.float32)
    lab_swap.wait_recv()

    def piece(s, r, f):
        return sums[s, r * rows : (r + 1) * rows, halves[f]]

    first = [[None, None] for _ in range(chips)]
    second = [[None, None] for _ in range(chips)]
    third = [None] * chips

    def add_sibling(s):
        theirs = members(s, sib_lab)
        for f in range(2):
            if s == 0:
                pts_swap[f].wait_recv()
            sums[s, :, halves[f]] += jnp.dot(
                theirs, sib_pts[:, halves[f]], preferred_element_type=jnp.float32
            )
            near = 1 + f
            out1[s, f, 0] = piece(s, near, f).astype(jnp.bfloat16)
            out1[s, f, 1] = piece(s, 3, f).astype(jnp.bfloat16)
            if s < 2:
                send_first(s, f)

    def send_first(s, f):
        first[s][f] = remote(
            out1.at[s, f], in1.at[s, f], s1_send.at[s, f], s1_recv.at[s, f], (x_id, y_id)[f]
        )

    def send_second(s):
        for f in range(2):
            first[s][f].wait_recv()
            far = 2 - f
            out2[s, f] = (piece(s, far, f) + in1[s, f, 1].astype(jnp.float32)).astype(jnp.bfloat16)
            second[s][f] = remote(
                out2.at[s, f], in2.at[s, f], s2_send.at[s, f], s2_recv.at[s, f], (y_id, x_id)[f]
            )

    def finish(s):
        whole = []
        for f in range(2):
            second[s][f].wait_recv()
            whole.append(
                piece(s, 0, f) + in1[s, f, 0].astype(jnp.float32) + in2[s, f].astype(jnp.float32)
            )
        return jnp.concatenate(whole, axis=1)

    def send_third(s):
        m = order[s]
        out3[m - 1] = finish(s).astype(jnp.bfloat16)
        third[m] = remote(
            out3.at[m - 1], in3.at[m - 1], s3_send.at[m - 1], s3_recv.at[m - 1], line_ids[m]
        )

    step = 128

    def make_unit(index):
        at = index * step
        ref, begin = (pts, at) if at < local else (sib_pts, at - local)
        wide = ref[begin : begin + step].astype(jnp.float32)
        mean = jnp.mean(wide * wide, axis=1, keepdims=True)
        unit = wide * lax.rsqrt(mean + EPSILON)
        unit_t[:, at : at + step] = unit.T.astype(jnp.bfloat16)

    units = 2 * local // step
    for s in range(chips):
        add_sibling(s)
    made = 0
    for s in range(chips):
        for _ in range(units // chips):
            make_unit(made)
            made += 1
        send_second(s)
        if s + 2 < chips:
            send_first(s + 2, 0)
            send_first(s + 2, 1)
        if s:
            send_third(s - 1)
    total = finish(chips - 1)
    for m in (2, 3, 1):
        third[m].wait_recv()
        total = total + in3[m - 1].astype(jnp.float32)
    mean = jnp.mean(total * total, axis=1, keepdims=True)
    grid[0, c] = (total * lax.rsqrt(mean + EPSILON)).astype(jnp.bfloat16)

    along = [None] * chips
    across = [[None] * QUAD for _ in range(chips)]

    def send_across(m):
        k = line[m]
        for r in (3, 1, 2):
            across[m][r] = remote(
                grid.at[0, k], grid.at[r, k], g2_send.at[m, r - 1], g2_recv.at[m, r - 1], quad_ids[r]
            )

    for m in (2, 1, 3):
        along[m] = remote(
            grid.at[0, c], grid.at[0, c], g1_send.at[m - 1], g1_recv.at[m - 1], line_ids[m]
        )
    send_across(0)
    for m in (1, 2, 3):
        along[m].wait_recv()
        send_across(m)

    def best_of(r):
        block = grid[r].reshape(K_HOST, features)
        scores = jnp.dot(block, unit_t[...], preferred_element_type=jnp.float32)
        return jnp.max(scores, axis=0, keepdims=True)

    quarter = features // chips
    columns = pl.ds(pl.multiple_of(c * quarter, quarter), quarter)
    for k in range(chips):
        cent_ref[k * rows : (k + 1) * rows, :] = grid[0, k, :, columns]
    best = best_of(0)
    for r in (1, 2, 3):
        for m in range(chips):
            across[m][r].wait_recv()
        best = jnp.maximum(best, best_of(r))

    best_out[...] = best[:, local:]
    last = remote(best_out, best_in, core_send.at[3], core_recv.at[3], sibling)
    for copy in started:
        copy.wait_send()
    last.wait_recv()
    near_ref[...] = 2.0 - 2.0 * jnp.maximum(best[:, :local], best_in[...]) / features


def window_body(points, assign):
    local, features = points.shape
    chips = lax.axis_size("chip")
    rows = K_HOST // chips
    half = features // 2
    vmem = pl.BlockSpec(memory_space=pltpu.VMEM)
    dma = pltpu.SemaphoreType.DMA
    pieces = [
        pltpu.VMEM((chips, 2, 2, rows, half), jnp.bfloat16),
        pltpu.VMEM((chips, 2, rows, half), jnp.bfloat16),
        pltpu.VMEM((chips - 1, rows, features), jnp.bfloat16),
    ]
    pairs = [(4,), (chips, 2), (chips, 2), (chips - 1,), (chips - 1,), (chips, 3)]
    centroids, nearest = pl.pallas_call(
        functools.partial(window_kernel, chips),
        out_shape=(
            jax.ShapeDtypeStruct((K_HOST, features // chips), jnp.bfloat16),
            jax.ShapeDtypeStruct((1, local), jnp.float32),
        ),
        in_specs=[vmem, vmem],
        out_specs=(vmem, vmem),
        scratch_shapes=[
            pltpu.VMEM((1, local), jnp.int32),
            pltpu.VMEM((local, features), jnp.bfloat16),
            pltpu.VMEM((chips, QUAD * rows, features), jnp.float32),
            *(buffer for buffer in pieces for _ in range(2)),
            pltpu.VMEM((QUAD, chips, rows, features), jnp.bfloat16),
            pltpu.VMEM((features, 2 * local), jnp.bfloat16),
            pltpu.VMEM((1, local), jnp.float32),
            pltpu.VMEM((1, local), jnp.float32),
            *(dma(shape) for shape in pairs for _ in range(2)),
        ],
        compiler_params=pltpu.CompilerParams(
            collective_id=0, has_side_effects=True, vmem_limit_bytes=48 * 1024 * 1024
        ),
    )(assign.reshape(1, local), points)
    return (centroids, nearest.reshape(local))


def solution(mesh):
    hosts, chips = mesh.shape["hst"], mesh.shape["chip"]
    fits = hosts == CYCLE and hosts == 2 * QUAD and chips == 4
    in_specs = (P(("hst", "chip"), None), P(("hst", "chip")))
    out_specs = (P("hst", "chip"), P(("hst", "chip")))
    return jax.shard_map(
        window_body if fits else general_body,
        mesh=mesh,
        in_specs=in_specs,
        out_specs=out_specs,
        check_vma=False,
    )
```

```python
import functools

import jax
import jax.numpy as jnp
from jax import lax
from jax.experimental import pallas as pl
from jax.experimental.pallas import tpu as pltpu
from jax.sharding import PartitionSpec as P

K_HOST = 128
CYCLE = 8


EPSILON = 1e-06
MESH = pl.DeviceIdType.MESH


def shifted(block, axis, distance):
    devices = range(lax.axis_size(axis))
    route = [((i - distance) % len(devices), i) for i in devices]
    return lax.ppermute(block, axis, route)


def cluster_sums(values, labels, row_count):
    stride = min(row_count, 1024)

    def one_block(offset):
        wanted = offset + jnp.arange(stride, dtype=jnp.int32)
        member = (wanted[:, None] == labels[None, :]).astype(jnp.bfloat16)
        return jnp.dot(member, values, preferred_element_type=jnp.float32)

    offsets = jnp.arange(row_count // stride, dtype=jnp.int32) * stride
    return lax.map(one_block, offsets).reshape(row_count, values.shape[1])


def general_body(points, assign):
    feature_count = points.shape[1]
    chip_count = lax.axis_size("chip")
    chip_index = lax.axis_index("chip")
    quarter = feature_count // chip_count
    host_points, host_labels = (
        lax.all_gather(points, "chip", axis=0, tiled=True),
        lax.all_gather(assign, "chip", axis=0, tiled=True),
    )
    columns = lax.dynamic_slice_in_dim(host_points, chip_index * quarter, quarter, 1)
    shares = lax.psum_scatter(
        cluster_sums(columns, host_labels, K_HOST * lax.axis_size("hst")),
        "hst",
        scatter_dimension=0,
        tiled=True,
    )
    squares = lax.psum(jnp.sum(shares * shares, axis=1), "chip")
    factor = lax.rsqrt(squares / feature_count + EPSILON)
    centroids = (shares * factor[:, None]).astype(jnp.bfloat16)
    own_block = lax.all_gather(centroids, "chip", axis=1, tiled=True)
    widened = points.astype(jnp.float32)
    unit_points = (
        widened * lax.rsqrt(jnp.mean(widened * widened, axis=1, keepdims=True) + EPSILON)
    ).astype(jnp.bfloat16)

    def nearest_in(candidates):
        scores = jnp.einsum(
            "pd,kd->pk", unit_points, candidates, preferred_element_type=jnp.float32
        )
        return jnp.min(2.0 - 2.0 * scores / feature_count, axis=1)

    nearest = nearest_in(own_block)
    moving = own_block
    for section_index in range(CYCLE - 1):
        moving = shifted(moving, "hst", 1)
        nearest = jnp.minimum(nearest, nearest_in(moving))
    return (centroids, nearest)


QUAD = 4


def window_kernel(
    chips,
    lab,
    pts,
    cent_ref,
    near_ref,
    sib_lab,
    sib_pts,
    sums,
    out1,
    in1,
    out2,
    in2,
    out3,
    in3,
    grid,
    unit_t,
    best_out,
    best_in,
    core_send,
    core_recv,
    s1_send,
    s1_recv,
    s2_send,
    s2_recv,
    s3_send,
    s3_recv,
    g1_send,
    g1_recv,
    g2_send,
    g2_recv,
):
    local, features = pts.shape
    rows = K_HOST // chips
    half = features // 2
    halves = (slice(0, half), slice(half, features))
    h = lax.axis_index("hst")
    c = lax.axis_index("chip")
    core = h % 2
    quad = h // 2
    qx, qy = quad % 2, quad // 2
    sibling = (h + 1 - 2 * core, c)
    quads = [quad, qy * 2 + (1 - qx), (1 - qy) * 2 + qx, (1 - qy) * 2 + (1 - qx)]
    quad_ids = [(q * 2 + core, c) for q in quads]
    x_id, y_id = quad_ids[1:3]
    line = [c, c + 1 - 2 * (c % 2), (c + 2) % 4, 3 - c]
    line_ids = [(h, k) for k in line]

    barrier = pltpu.get_barrier_semaphore()
    partners = [sibling] + quad_ids[1:] + line_ids[1:]
    for partner in partners:
        pl.semaphore_signal(barrier, inc=1, device_id=partner, device_id_type=MESH)
    pl.semaphore_wait(barrier, len(partners))

    started = []

    def remote(src, dst, send, recv, device):
        copy = pltpu.make_async_remote_copy(
            src_ref=src,
            dst_ref=dst,
            send_sem=send,
            recv_sem=recv,
            device_id=device,
            device_id_type=MESH,
        )
        copy.start()
        started.append(copy)
        return copy

    lab_swap = remote(lab, sib_lab, core_send.at[0], core_recv.at[0], sibling)
    pts_swap = [
        remote(
            pts.at[:, halves[f]], sib_pts.at[:, halves[f]], core_send.at[1 + f], core_recv.at[1 + f], sibling
        )
        for f in range(2)
    ]

    order = (2, 3, 1, 0)
    row = lax.broadcasted_iota(jnp.int32, (QUAD * rows, local), 0)
    part, within = row // rows, row % rows
    base = jnp.zeros_like(row)
    for r in range(QUAD):
        base = jnp.where(part == r, (quads[r] * 2 + core) * K_HOST, base)
    base = base + within

    def members(s, labels):
        return (base + line[order[s]] * rows == labels[...]).astype(jnp.bfloat16)

    for s in range(chips):
        sums[s] = jnp.dot(members(s, lab), pts[...], preferred_element_type=jnp.float32)
    lab_swap.wait_recv()

    def piece(s, r, f):
        return sums[s, r * rows : (r + 1) * rows, halves[f]]

    first = [[None, None] for _ in range(chips)]
    second = [[None, None] for _ in range(chips)]
    third = [None] * chips

    def add_sibling(s):
        theirs = members(s, sib_lab)
        for f in range(2):
            if s == 0:
                pts_swap[f].wait_recv()
            sums[s, :, halves[f]] += jnp.dot(
                theirs, sib_pts[:, halves[f]], preferred_element_type=jnp.float32
            )
            near = 1 + f
            out1[s, f, 0] = piece(s, near, f).astype(jnp.bfloat16)
            out1[s, f, 1] = piece(s, 3, f).astype(jnp.bfloat16)
            if s < 2:
                send_first(s, f)

    def send_first(s, f):
        first[s][f] = remote(
            out1.at[s, f], in1.at[s, f], s1_send.at[s, f], s1_recv.at[s, f], (x_id, y_id)[f]
        )

    def send_second(s):
        for f in range(2):
            first[s][f].wait_recv()
            far = 2 - f
            out2[s, f] = (piece(s, far, f) + in1[s, f, 1].astype(jnp.float32)).astype(jnp.bfloat16)
            second[s][f] = remote(
                out2.at[s, f], in2.at[s, f], s2_send.at[s, f], s2_recv.at[s, f], (y_id, x_id)[f]
            )

    def finish(s):
        whole = []
        for f in range(2):
            second[s][f].wait_recv()
            whole.append(
                piece(s, 0, f) + in1[s, f, 0].astype(jnp.float32) + in2[s, f].astype(jnp.float32)
            )
        return jnp.concatenate(whole, axis=1)

    def send_third(s):
        m = order[s]
        out3[m - 1] = finish(s).astype(jnp.bfloat16)
        third[m] = remote(
            out3.at[m - 1], in3.at[m - 1], s3_send.at[m - 1], s3_recv.at[m - 1], line_ids[m]
        )

    step = 128

    def make_unit(index):
        at = index * step
        ref, begin = (pts, at) if at < local else (sib_pts, at - local)
        wide = ref[begin : begin + step].astype(jnp.float32)
        mean = jnp.mean(wide * wide, axis=1, keepdims=True)
        unit = wide * lax.rsqrt(mean + EPSILON)
        unit_t[:, at : at + step] = unit.T.astype(jnp.bfloat16)

    units = 2 * local // step
    for s in range(chips):
        add_sibling(s)
    made = 0
    for s in range(chips):
        send_second(s)
        if s + 2 < chips:
            send_first(s + 2, 0)
            send_first(s + 2, 1)
        for _ in range(units // chips):
            make_unit(made)
            made += 1
        if s:
            send_third(s - 1)
    total = finish(chips - 1)
    for m in (2, 3, 1):
        third[m].wait_recv()
        total = total + in3[m - 1].astype(jnp.float32)
    mean = jnp.mean(total * total, axis=1, keepdims=True)
    grid[0, c] = (total * lax.rsqrt(mean + EPSILON)).astype(jnp.bfloat16)

    along = [None] * chips
    across = [[None] * QUAD for _ in range(chips)]

    def send_across(m):
        k = line[m]
        for r in (3, 1, 2):
            across[m][r] = remote(
                grid.at[0, k], grid.at[r, k], g2_send.at[m, r - 1], g2_recv.at[m, r - 1], quad_ids[r]
            )

    for m in (2, 1, 3):
        along[m] = remote(
            grid.at[0, c], grid.at[0, c], g1_send.at[m - 1], g1_recv.at[m - 1], line_ids[m]
        )
    send_across(0)
    for m in (1, 2, 3):
        along[m].wait_recv()
        send_across(m)

    def best_of(r):
        block = grid[r].reshape(K_HOST, features)
        scores = jnp.dot(block, unit_t[...], preferred_element_type=jnp.float32)
        return jnp.max(scores, axis=0, keepdims=True)

    quarter = features // chips
    columns = pl.ds(pl.multiple_of(c * quarter, quarter), quarter)
    for k in range(chips):
        cent_ref[k * rows : (k + 1) * rows, :] = grid[0, k, :, columns]
    best = best_of(0)
    for r in (1, 2, 3):
        for m in range(chips):
            across[m][r].wait_recv()
        best = jnp.maximum(best, best_of(r))

    best_out[...] = best[:, local:]
    last = remote(best_out, best_in, core_send.at[3], core_recv.at[3], sibling)
    for copy in started:
        copy.wait_send()
    last.wait_recv()
    near_ref[...] = 2.0 - 2.0 * jnp.maximum(best[:, :local], best_in[...]) / features


def window_body(points, assign):
    local, features = points.shape
    chips = lax.axis_size("chip")
    rows = K_HOST // chips
    half = features // 2
    vmem = pl.BlockSpec(memory_space=pltpu.VMEM)
    dma = pltpu.SemaphoreType.DMA
    pieces = [
        pltpu.VMEM((chips, 2, 2, rows, half), jnp.bfloat16),
        pltpu.VMEM((chips, 2, rows, half), jnp.bfloat16),
        pltpu.VMEM((chips - 1, rows, features), jnp.bfloat16),
    ]
    pairs = [(4,), (chips, 2), (chips, 2), (chips - 1,), (chips - 1,), (chips, 3)]
    centroids, nearest = pl.pallas_call(
        functools.partial(window_kernel, chips),
        out_shape=(
            jax.ShapeDtypeStruct((K_HOST, features // chips), jnp.bfloat16),
            jax.ShapeDtypeStruct((1, local), jnp.float32),
        ),
        in_specs=[vmem, vmem],
        out_specs=(vmem, vmem),
        scratch_shapes=[
            pltpu.VMEM((1, local), jnp.int32),
            pltpu.VMEM((local, features), jnp.bfloat16),
            pltpu.VMEM((chips, QUAD * rows, features), jnp.float32),
            *(buffer for buffer in pieces for _ in range(2)),
            pltpu.VMEM((QUAD, chips, rows, features), jnp.bfloat16),
            pltpu.VMEM((features, 2 * local), jnp.bfloat16),
            pltpu.VMEM((1, local), jnp.float32),
            pltpu.VMEM((1, local), jnp.float32),
            *(dma(shape) for shape in pairs for _ in range(2)),
        ],
        compiler_params=pltpu.CompilerParams(
            collective_id=0, has_side_effects=True, vmem_limit_bytes=48 * 1024 * 1024
        ),
    )(assign.reshape(1, local), points)
    return (centroids, nearest.reshape(local))


def solution(mesh):
    hosts, chips = mesh.shape["hst"], mesh.shape["chip"]
    fits = hosts == CYCLE and hosts == 2 * QUAD and chips == 4
    in_specs = (P(("hst", "chip"), None), P(("hst", "chip")))
    out_specs = (P("hst", "chip"), P(("hst", "chip")))
    return jax.shard_map(
        window_body if fits else general_body,
        mesh=mesh,
        in_specs=in_specs,
        out_specs=out_specs,
        check_vma=False,
    )
```
